32 devices in a mesh: segment: 4 (over z), seq: 8 (over y, x, core).
Axes of the slice: x: 2, y: 2, z: 4, core: 2. Of those that a mesh axis runs over, the one named last changes fastest.
Arguments:
- queries: bfloat16 [4, 4096, 8192], P('segment', 'seq'), may hold values from -40 to 40
- keys_in: bfloat16 [4, 4096, 1024], P('segment', 'seq'), may hold values from -6 to 6
- values_in: bfloat16 [4, 4096, 1024], P('segment', 'seq'), may hold values from -6 to 6
- random_blocks: int32 [4, 64, 3], P('segment', 'seq'), may hold values from 0 to 63, as said below
- global_blocks: int32 [4, 2], P('segment'), may hold values from 0 to 63
Outputs:
- handed: bfloat16 [4, 4096, 8192], P('segment', 'seq')
The draws below stay inside these ranges and needn't reach their ends.
Inputs may be any that keep to these rules, and one draw needn't show every extreme that they name: random_blocks[s, j] are block numbers; the rows of one device of seq name at most 3 blocks lying on any single device of seq, and in every section one device of seq is named exactly once by the rows of every device.
All inputs are finite; a program needn't handle non-finite values.
Results may differ from the reference program's by a relative error of at most 0.0049.
Values may be sent and summed in bfloat16 or wider, within the bound.
A program may use at most 128 MiB of HBM per device.

```python
import jax
import jax.numpy as jnp
from jax import lax

HEADS = 64
KV_HEADS = 8
HEAD = 128
BLOCK = 64
GLOB = 2
RAND = 3
TOK_DEV = 512
SEGMENTS = 4
TOKENS = 4096
BLK_DEV = 8
NBLK = 64
CAP = 3
KEYS = 512


def shared_noise(key):
    shape = (SEGMENTS, TOKENS, KV_HEADS * HEAD)
    gauss = jax.random.normal(jax.random.fold_in(key, 101), shape, jnp.float32)
    return gauss


def draw_keys_in(key, part):
    gauss = shared_noise(key)
    key_rows = jnp.clip(gauss, -6.0, 6.0)
    return key_rows.astype(jnp.bfloat16)


def draw_queries(key, part):
    key = jax.random.fold_in(key, 2)
    shape = (SEGMENTS, TOKENS, HEADS * HEAD)
    result = jnp.clip(2.0 * jax.random.normal(key, shape, jnp.float32), -8.0, 8.0)
    return result.astype(jnp.bfloat16)


def draw_random_blocks(key, part):
    key = jax.random.fold_in(key, 5)
    number_of_strings = TOKENS // TOK_DEV
    wanted = BLK_DEV * RAND
    tile_locations = number_of_strings * CAP
    holder_processor = jnp.arange(tile_locations, dtype=jnp.int32) // CAP
    sorted_ordinals = jnp.arange(tile_locations, dtype=jnp.int32)

    def one_segment(segment_key):
        foremost_tile, second, third = jax.random.split(segment_key, 3)
        preference_increment = jax.random.randint(foremost_tile, (number_of_strings,), 0, 4)
        picked_tile_flags = jax.random.randint(second, (), 0, number_of_strings)

        def one_device(device_key):
            noise_key, shuffle_key, local_key = jax.random.split(device_key, 3)
            stochastic_perturbation = jax.random.randint(noise_key, (tile_locations,), 0, 16384)
            raw_affinity_table = (preference_increment[holder_processor] * 16384 + stochastic_perturbation + jnp.where(holder_processor == picked_tile_flags, 131072, 0)) * tile_locations + sorted_ordinals
            chosen = lax.top_k(raw_affinity_table, wanted)[1]
            owners = jax.random.permutation(shuffle_key, holder_processor[chosen])
            local = jax.random.randint(local_key, (wanted,), 0, BLK_DEV)
            return (owners * BLK_DEV + local).reshape(BLK_DEV, RAND)
        per_device = jax.vmap(one_device)(jax.random.split(third, number_of_strings))
        return per_device.reshape(NBLK, RAND)
    return jax.vmap(one_segment)(jax.random.split(key, SEGMENTS)).astype(jnp.int32)


def with_ends(drawn, key, least, largest):
    longest = drawn.shape.index(max(drawn.shape))
    spots = []
    for shift in (0, 1):
        where = [jax.random.randint(jax.random.fold_in(key, axis), (), 0, length) for axis, length in enumerate(drawn.shape)]
        where[longest] = (where[longest] + shift) % drawn.shape[longest]
        spots.append(tuple(where))
    return drawn.at[spots[0]].set(least).at[spots[1]].set(largest)


def shard_levels(rng, shape, cuts, least, largest):
    factor_of = 1.0
    for axis_at, shards_of in cuts:
        heights = jax.random.uniform(jax.random.fold_in(jax.random.fold_in(rng, 6), axis_at), (shards_of,), jnp.float32, least / len(cuts), largest / len(cuts))
        factor_of = factor_of * jnp.repeat(jnp.exp(heights), shape[axis_at] // shards_of).reshape((-1,) + (1,) * (len(shape) - 1 - axis_at))
    return factor_of


def normal_values(key, dims, spread, reach, shards=(), kind=jnp.bfloat16):
    values = jax.random.normal(key, dims, jnp.float32) * spread
    if len(shards) > 0:
        values = shard_levels(key, dims, shards, -0.22, 0.18) * values
    return jnp.clip(values, min=-reach, max=reach).astype(kind)


def setup_inputs(seed: int = 0) -> dict:
    keys = jax.random.split(jax.random.key(seed), 6)
    return {
        "queries": draw_queries(jax.random.fold_in(keys[5], 71), 0),
        "keys_in": draw_keys_in(jax.random.fold_in(keys[5], 71), 0),
        "values_in": normal_values(keys[2], (SEGMENTS, TOKENS, KV_HEADS * HEAD), 1.0, 6.0, ((0, 4), (1, 8))),
        "random_blocks": draw_random_blocks(jax.random.fold_in(keys[5], 71), 0),
        "global_blocks": with_ends(jax.random.randint(keys[4], (SEGMENTS, GLOB), 0, NBLK), jax.random.fold_in(keys[4], 1), 0, NBLK - 1).astype(jnp.int32),
    }


def attend(query_rows, key_rows, value_rows, random_rows, global_row):
    nblk = query_rows.shape[0] // BLOCK
    kvw = key_rows.shape[1]
    group = HEADS // KV_HEADS
    stacked = jnp.concatenate([key_rows, value_rows], axis=-1).reshape(nblk, BLOCK, 2 * kvw)
    query_blocks = query_rows.reshape(nblk, BLOCK, KV_HEADS, group, HEAD)
    scale = 1.0 / (HEAD ** 0.5)

    def one_row(j):
        listed = jnp.concatenate([j + jnp.array([-1, 0, 1], jnp.int32), global_row, random_rows[j]]).astype(jnp.int32)
        valid = jnp.concatenate([jnp.stack([j >= 1, j >= 0, j + 1 < nblk]), jnp.ones((GLOB + RAND,), bool)])
        picked = stacked[jnp.clip(listed, 0, nblk - 1)].reshape(KEYS, 2 * kvw)
        key_portion = picked[:, :kvw].reshape(KEYS, KV_HEADS, HEAD).astype(jnp.float32)
        value_portion = picked[:, kvw:].reshape(KEYS, KV_HEADS, HEAD).astype(jnp.float32)
        query_portion = query_blocks[j].astype(jnp.float32)
        scores = jnp.einsum('qhgd,khd->hgqk', query_portion, key_portion) * scale
        mask = jnp.repeat(valid, BLOCK)
        scores = jnp.where(mask[None, None, None, :], scores, -jnp.inf)
        top = jnp.max(scores, axis=-1, keepdims=True)
        expo = jnp.exp(scores - top)
        attention_probs = (expo / jnp.sum(expo, axis=-1, keepdims=True)).astype(jnp.bfloat16)
        attention_probs = lax.optimization_barrier(attention_probs).astype(jnp.float32)
        result = jnp.einsum('hgqk,khd->qhgd', attention_probs, value_portion)
        return result.astype(jnp.bfloat16).reshape(BLOCK, HEADS * HEAD)

    rows = lax.map(one_row, jnp.arange(nblk, dtype=jnp.int32))
    return rows.reshape(nblk * BLOCK, HEADS * HEAD)


def reference(queries, keys_in, values_in, random_blocks, global_blocks):
    sections = []
    for section in range(queries.shape[0]):
        sections.append(attend(queries[section], keys_in[section], values_in[section], random_blocks[section], global_blocks[section]))
    attended = jnp.stack(sections)
    return jnp.roll(attended, 1, axis=0)
```

```python
import functools
import math

import jax
import jax.numpy as jnp
from jax import lax
from jax.experimental import pallas as pl
from jax.experimental.pallas import tpu as pltpu
from jax.sharding import PartitionSpec as P

HEAD = 128
BLOCK = 64
GLOB = 2
RAND = 3
MESH = pl.DeviceIdType.MESH
SLOT_BYTES = 16 * 1024 * 1024


def kernel(
    n, segs, kvh, slots, ahead,
    rand_ref, glob_ref, q_ref, k_ref, v_ref, out_ref,
    q_buf, res, *rest,
):
    kv = rest[:slots]
    q_sem, own_sem, send_sem, recv_sem, fsend, frecv, zsend, zrecv, free_c, free_p = rest[slots:]
    tok = q_ref.shape[1]
    group = q_ref.shape[2] // (kvh * HEAD)
    gw = group * HEAD
    blk_dev = tok // BLOCK
    nblk = blk_dev * n
    chips = n // 2
    me = lax.axis_index("seq")
    seg = lax.axis_index("segment")
    chip, core = me // 2, me % 2
    partner = chip * 2 + (1 - core)
    after, before = (seg + 1) % segs, (seg + segs - 1) % segs
    others = [(chip + o) % chips for o in range(1, chips)]

    def q_copy(h):
        return pltpu.make_async_copy(
            q_ref.at[0, :, pl.ds(h * gw, gw)], q_buf.at[h], q_sem.at[h]
        )

    def place(s, c, i):
        return kv[s].at[pl.ds((core * 2 + i) * chips * blk_dev + c * blk_dev, blk_dev)]

    def own_copy(h, i):
        src = (k_ref, v_ref)[i].at[:, :, pl.ds(h * HEAD, HEAD)]
        return pltpu.make_async_copy(src, place(h % slots, chip, i), own_sem.at[h % slots, i])

    def peer_copy(h, c, i):
        s = h % slots
        src = (k_ref, v_ref)[i].at[:, :, pl.ds(h * HEAD, HEAD)]
        return pltpu.make_async_remote_copy(
            src_ref=src, dst_ref=place(s, chip, i),
            send_sem=send_sem.at[s, c, i], recv_sem=recv_sem.at[s, chip, i],
            device_id={"seq": c * 2 + core}, device_id_type=MESH,
        )

    def peer_arrival(h, c, i):
        s = h % slots
        src = (k_ref, v_ref)[i].at[:, :, pl.ds(h * HEAD, HEAD)]
        return pltpu.make_async_remote_copy(
            src_ref=src, dst_ref=place(s, c, i),
            send_sem=send_sem.at[s, c, i], recv_sem=recv_sem.at[s, c, i],
            device_id={"seq": c * 2 + core}, device_id_type=MESH,
        )

    def forward(h, half):
        s = h % slots
        part = kv[s].at[pl.ds(half * 2 * chips * blk_dev, 2 * chips * blk_dev)]
        return pltpu.make_async_remote_copy(
            src_ref=part, dst_ref=part,
            send_sem=fsend.at[s], recv_sem=frecv.at[s],
            device_id={"seq": partner}, device_id_type=MESH,
        )

    def start_gather(h):
        if h >= slots:
            pl.semaphore_wait(free_c.at[h % slots], chips - 1)
        for i in range(2):
            for c in others:
                peer_copy(h, c, i).start()
            own_copy(h, i).start()

    barrier = pltpu.get_barrier_semaphore()
    greeted = [{"seq": c * 2 + core} for c in others]
    greeted += [{"seq": partner}, {"segment": after}, {"segment": before}]
    for who in greeted:
        pl.semaphore_signal(barrier, inc=1, device_id=who, device_id_type=MESH)
    q_copy(0).start()
    pl.semaphore_wait(barrier, len(greeted))

    for h in range(min(ahead, slots, kvh)):
        start_gather(h)
    for h in range(1, kvh):
        q_copy(h).start()

    scale = 1.0 / math.sqrt(HEAD)
    column = lax.broadcasted_iota(jnp.int32, (1, (3 + GLOB + RAND) * BLOCK), 1)

    for h in range(kvh):
        s = h % slots
        for i in range(2):
            own_copy(h, i).wait()
            for c in others:
                peer_arrival(h, c, i).wait_recv()
        if h >= slots:
            pl.semaphore_wait(free_p.at[s], 1)
        forward(h, core).start()
        if ahead <= slots and h + ahead < kvh and h + ahead < slots:
            start_gather(h + ahead)
        q_copy(h).wait()
        forward(h, 1 - core).wait_recv()

        def block_step(j, carry, h=h, s=s):
            row = me * blk_dev + j
            listed = [jnp.maximum(row - 1, 0), row, jnp.minimum(row + 1, nblk - 1)]
            listed += [glob_ref[0, i] for i in range(GLOB)]
            listed += [rand_ref[0, j, i] for i in range(RAND)]

            def picked(i):
                parts = []
                for b in listed:
                    dev = lax.div(b, blk_dev)
                    where = (lax.rem(dev, 2) * 2 + i) * chips + lax.div(dev, 2)
                    parts.append(kv[s][where * blk_dev + lax.rem(b, blk_dev)])
                return jnp.concatenate(parts, axis=0)

            rows = pl.ds(pl.multiple_of(j * BLOCK, BLOCK), BLOCK)
            q_rows = q_buf[h, rows, :]
            q = jnp.concatenate([q_rows[:, g * HEAD : (g + 1) * HEAD] for g in range(group)], axis=0)
            scores = lax.dot_general(
                q, picked(0), (((1,), (1,)), ((), ())), preferred_element_type=jnp.float32
            )
            listed_here = ((column >= BLOCK) | (row >= 1)) & (
                (column < 2 * BLOCK) | (column >= 3 * BLOCK) | (row + 1 < nblk)
            )
            scores = scores * scale + jnp.where(listed_here, 0.0, -jnp.inf)
            top = jnp.max(scores, axis=-1, keepdims=True)
            expo = jnp.exp(scores - top)
            weights = (expo * (1.0 / jnp.sum(expo, axis=-1, keepdims=True))).astype(jnp.bfloat16)
            result = jnp.dot(weights, picked(1), preferred_element_type=jnp.float32)
            result = result.astype(jnp.bfloat16)
            for g in range(group):
                res[h, rows, pl.ds(g * HEAD, HEAD)] = result[g * BLOCK : (g + 1) * BLOCK, :]
            pltpu.make_async_remote_copy(
                src_ref=res.at[h, rows, :],
                dst_ref=out_ref.at[0, rows, pl.ds(h * gw, gw)],
                send_sem=zsend.at[h], recv_sem=zrecv.at[h],
                device_id={"segment": after}, device_id_type=MESH,
            ).start()
            return carry

        lax.fori_loop(0, blk_dev, block_step, 0)

        for i in range(2):
            for c in others:
                peer_copy(h, c, i).wait_send()
        forward(h, core).wait_send()
        if h + slots < kvh:
            for c in others:
                pl.semaphore_signal(
                    free_c.at[s], inc=1, device_id={"seq": c * 2 + core}, device_id_type=MESH
                )
            pl.semaphore_signal(
                free_p.at[s], inc=1, device_id={"seq": partner}, device_id_type=MESH
            )
            start_gather(h + slots)

    for h in range(kvh):
        pltpu.make_async_remote_copy(
            src_ref=res.at[h],
            dst_ref=out_ref.at[0, :, pl.ds(h * gw, gw)],
            send_sem=zsend.at[h], recv_sem=zrecv.at[h],
            device_id={"segment": after}, device_id_type=MESH,
        ).wait()


def per_device(queries, keys_in, values_in, random_blocks, global_blocks):
    n, segs = lax.axis_size("seq"), lax.axis_size("segment")
    tok, width = queries.shape[1:]
    kvh = keys_in.shape[2] // HEAD
    gw = width // kvh
    chips = n // 2
    slots = min(kvh, max(2, SLOT_BYTES // (4 * n * tok * HEAD)))
    anywhere = pl.BlockSpec(memory_space=pl.ANY)
    scalars = pl.BlockSpec(memory_space=pltpu.SMEM)
    keys = (3 + GLOB + RAND) * BLOCK
    keys_in, values_in = (x.reshape(tok // BLOCK, BLOCK, kvh * HEAD) for x in (keys_in, values_in))
    return pl.pallas_call(
        functools.partial(kernel, n, segs, kvh, slots, min(2, slots)),
        out_shape=jax.ShapeDtypeStruct(queries.shape, jnp.bfloat16),
        in_specs=[scalars, scalars, anywhere, anywhere, anywhere],
        out_specs=anywhere,
        scratch_shapes=[
            pltpu.VMEM((kvh, tok, gw), jnp.bfloat16),
            pltpu.VMEM((kvh, tok, gw), jnp.bfloat16),
            *[pltpu.VMEM((4 * chips * tok // BLOCK, BLOCK, HEAD), jnp.bfloat16) for _ in range(slots)],
            pltpu.SemaphoreType.DMA((kvh,)),
            pltpu.SemaphoreType.DMA((slots, 2)),
            pltpu.SemaphoreType.DMA((slots, chips, 2)),
            pltpu.SemaphoreType.DMA((slots, chips, 2)),
            pltpu.SemaphoreType.DMA((slots,)),
            pltpu.SemaphoreType.DMA((slots,)),
            pltpu.SemaphoreType.DMA((kvh,)),
            pltpu.SemaphoreType.DMA((kvh,)),
            pltpu.SemaphoreType.REGULAR((slots,)),
            pltpu.SemaphoreType.REGULAR((slots,)),
        ],
        compiler_params=pltpu.CompilerParams(
            collective_id=0, has_side_effects=True, vmem_limit_bytes=56 * 1024 * 1024
        ),
        cost_estimate=pl.CostEstimate(
            flops=4 * tok * width * keys,
            bytes_accessed=4 * tok * width,
            transcendentals=tok * width // HEAD * keys,
        ),
    )(random_blocks, global_blocks, queries, keys_in, values_in)


def solution(mesh):
    in_specs = (
        P("segment", "seq", None),
        P("segment", "seq", None),
        P("segment", "seq", None),
        P("segment", "seq", None),
        P("segment", None),
    )
    out_specs = P("segment", "seq", None)
    return jax.shard_map(
        per_device, mesh=mesh, in_specs=in_specs, out_specs=out_specs, check_vma=False
    )
```

```python
import functools
import math

import jax
import jax.numpy as jnp
from jax import lax
from jax.experimental import pallas as pl
from jax.experimental.pallas import tpu as pltpu
from jax.sharding import PartitionSpec as P

HEAD = 128
BLOCK = 64
GLOB = 2
RAND = 3
MESH = pl.DeviceIdType.MESH
SLOT_BYTES = 16 * 1024 * 1024


def kernel(
    n, segs, kvh, slots, ahead,
    rand_ref, glob_ref, rand_hbm, glob_hbm, q_ref, k_ref, v_ref, out_ref,
    q_buf, res, rand_in, glob_in, rand_moved, glob_moved, *rest,
):
    kv = rest[: slots + 1]
    (
        q_sem, own_sem, send_sem, recv_sem, fsend, frecv,
        zsend, zrecv, ship_send, ship_recv, table_sem, free_c, free_p,
    ) = rest[slots + 1 :]
    tok = q_ref.shape[1]
    group = q_ref.shape[2] // (kvh * HEAD)
    gw = group * HEAD
    blk_dev = tok // BLOCK
    nblk = blk_dev * n
    chips = n // 2
    moved = kvh - 1
    me = lax.axis_index("seq")
    seg = lax.axis_index("segment")
    chip, core = me // 2, me % 2
    partner = chip * 2 + (1 - core)
    after, before = (seg + 1) % segs, (seg + segs - 1) % segs
    others = [(chip + o) % chips for o in range(1, chips)]

    def slot(h):
        return slots if h == moved else h % slots

    def q_copy(h):
        return pltpu.make_async_copy(
            q_ref.at[0, :, pl.ds(h * gw, gw)], q_buf.at[h], q_sem.at[h]
        )

    def place(s, c, i):
        return kv[s].at[pl.ds((core * 2 + i) * chips * blk_dev + c * blk_dev, blk_dev)]

    def own_rows(h, i):
        return (k_ref, v_ref)[i].at[:, :, pl.ds(h * HEAD, HEAD)]

    def own_copy(h, i):
        return pltpu.make_async_copy(
            own_rows(h, i), place(slot(h), chip, i), own_sem.at[slot(h), i]
        )

    def peer_copy(h, c, i):
        s = slot(h)
        return pltpu.make_async_remote_copy(
            src_ref=place(s, chip, i) if h == moved else own_rows(h, i),
            dst_ref=place(s, chip, i),
            send_sem=send_sem.at[s, c, i], recv_sem=recv_sem.at[s, chip, i],
            device_id={"seq": c * 2 + core}, device_id_type=MESH,
        )

    def peer_arrival(h, c, i):
        s = slot(h)
        return pltpu.make_async_remote_copy(
            src_ref=place(s, c, i), dst_ref=place(s, c, i),
            send_sem=send_sem.at[s, c, i], recv_sem=recv_sem.at[s, c, i],
            device_id={"seq": c * 2 + core}, device_id_type=MESH,
        )

    def forward(h, half):
        s = slot(h)
        part = kv[s].at[pl.ds(half * 2 * chips * blk_dev, 2 * chips * blk_dev)]
        return pltpu.make_async_remote_copy(
            src_ref=part, dst_ref=part,
            send_sem=fsend.at[s], recv_sem=frecv.at[s],
            device_id={"seq": partner}, device_id_type=MESH,
        )

    def ship(src, dst, k):
        return pltpu.make_async_remote_copy(
            src_ref=src, dst_ref=dst, send_sem=ship_send.at[k], recv_sem=ship_recv.at[k],
            device_id={"segment": after}, device_id_type=MESH,
        )

    shipped = [ship(own_rows(moved, i), place(slots, chip, i), i) for i in range(2)]
    shipped += [ship(rand_hbm, rand_in, 2), ship(glob_hbm, glob_in, 3)]
    shipped.append(ship(q_ref.at[0, :, pl.ds(moved * gw, gw)], q_buf.at[moved], 4))
    list_copies = [
        pltpu.make_async_copy(rand_in, rand_moved, table_sem.at[0]),
        pltpu.make_async_copy(glob_in, glob_moved, table_sem.at[1]),
    ]

    def start_gather(h):
        if slots <= h < moved:
            pl.semaphore_wait(free_c.at[h % slots], chips - 1)
        for i in range(2):
            if h == moved:
                shipped[i].wait_recv()
            for c in others:
                peer_copy(h, c, i).start()
            if h < moved:
                own_copy(h, i).start()

    barrier = pltpu.get_barrier_semaphore()
    greeted = [{"seq": c * 2 + core} for c in others]
    greeted += [{"seq": partner}, {"segment": after}, {"segment": before}]
    for who in greeted:
        pl.semaphore_signal(barrier, inc=1, device_id=who, device_id_type=MESH)
    q_copy(0).start()
    pl.semaphore_wait(barrier, len(greeted))

    start_gather(0)
    for copy in shipped:
        copy.start()
    for h in range(1, ahead):
        start_gather(h)
    for h in range(1, moved):
        q_copy(h).start()

    scale = 1.0 / math.sqrt(HEAD)
    column = lax.broadcasted_iota(jnp.int32, (1, (3 + GLOB + RAND) * BLOCK), 1)

    for h in range(kvh):
        s = slot(h)
        for i in range(2):
            if h < moved:
                own_copy(h, i).wait()
            for c in others:
                peer_arrival(h, c, i).wait_recv()
        if slots <= h < moved:
            pl.semaphore_wait(free_p.at[s], 1)
        forward(h, core).start()
        if h + ahead < slots:
            start_gather(h + ahead)
        if h + ahead == moved:
            start_gather(moved)
        if h < moved:
            q_copy(h).wait()
        else:
            for arrival, copy in zip(shipped[2:4], list_copies):
                arrival.wait_recv()
                copy.start()
            for copy in list_copies:
                copy.wait()
            shipped[4].wait_recv()
        forward(h, 1 - core).wait_recv()

        def block_step(j, carry, h=h, s=s):
            rand, glob = (rand_ref, glob_ref) if h < moved else (rand_moved, glob_moved)
            row = me * blk_dev + j
            listed = [jnp.maximum(row - 1, 0), row, jnp.minimum(row + 1, nblk - 1)]
            listed += [glob[0, i] for i in range(GLOB)] + [rand[i, 0, j] for i in range(RAND)]

            def picked(i):
                parts = []
                for b in listed:
                    dev = lax.div(b, blk_dev)
                    where = (lax.rem(dev, 2) * 2 + i) * chips + lax.div(dev, 2)
                    parts.append(kv[s][where * blk_dev + lax.rem(b, blk_dev)])
                return jnp.concatenate(parts, axis=0)

            rows = pl.ds(pl.multiple_of(j * BLOCK, BLOCK), BLOCK)
            q_rows = q_buf[h, rows, :]
            q = jnp.concatenate([q_rows[:, g * HEAD : (g + 1) * HEAD] for g in range(group)], axis=0)
            scores = lax.dot_general(
                q, picked(0), (((1,), (1,)), ((), ())), preferred_element_type=jnp.float32
            )
            listed_here = ((column >= BLOCK) | (row >= 1)) & (
                (column < 2 * BLOCK) | (column >= 3 * BLOCK) | (row + 1 < nblk)
            )
            scores = scores * scale + jnp.where(listed_here, 0.0, -jnp.inf)
            top = jnp.max(scores, axis=-1, keepdims=True)
            expo = jnp.exp(scores - top)
            weights = (expo * (1.0 / jnp.sum(expo, axis=-1, keepdims=True))).astype(jnp.bfloat16)
            result = jnp.dot(weights, picked(1), preferred_element_type=jnp.float32)
            result = result.astype(jnp.bfloat16)
            for g in range(group):
                piece = result[g * BLOCK : (g + 1) * BLOCK, :]
                if h < moved:
                    res[h, rows, pl.ds(g * HEAD, HEAD)] = piece
                else:
                    out_ref[0, rows, pl.ds(h * gw + g * HEAD, HEAD)] = piece
            if h < moved:
                pltpu.make_async_remote_copy(
                    src_ref=res.at[h, rows, :],
                    dst_ref=out_ref.at[0, rows, pl.ds(h * gw, gw)],
                    send_sem=zsend.at[h], recv_sem=zrecv.at[h],
                    device_id={"segment": after}, device_id_type=MESH,
                ).start()
            return carry

        lax.fori_loop(0, blk_dev, block_step, 0)

        for i in range(2):
            for c in others:
                peer_copy(h, c, i).wait_send()
        forward(h, core).wait_send()
        if h + slots < moved:
            for c in others:
                pl.semaphore_signal(
                    free_c.at[s], inc=1, device_id={"seq": c * 2 + core}, device_id_type=MESH
                )
            pl.semaphore_signal(
                free_p.at[s], inc=1, device_id={"seq": partner}, device_id_type=MESH
            )
            start_gather(h + slots)

    for copy in shipped:
        copy.wait_send()
    for h in range(moved):
        pltpu.make_async_remote_copy(
            src_ref=res.at[h],
            dst_ref=out_ref.at[0, :, pl.ds(h * gw, gw)],
            send_sem=zsend.at[h], recv_sem=zrecv.at[h],
            device_id={"segment": after}, device_id_type=MESH,
        ).wait()


def per_device(queries, keys_in, values_in, random_blocks, global_blocks):
    n, segs = lax.axis_size("seq"), lax.axis_size("segment")
    tok, width = queries.shape[1:]
    kvh = keys_in.shape[2] // HEAD
    gw = width // kvh
    chips = n // 2
    blk_dev = tok // BLOCK
    slots = min(kvh - 1, max(2, SLOT_BYTES // (4 * n * tok * HEAD)))
    anywhere = pl.BlockSpec(memory_space=pl.ANY)
    scalars = pl.BlockSpec(memory_space=pltpu.SMEM)
    keys = (3 + GLOB + RAND) * BLOCK
    keys_in, values_in = (x.reshape(blk_dev, BLOCK, kvh * HEAD) for x in (keys_in, values_in))
    random_blocks = jnp.transpose(random_blocks, (2, 0, 1))
    return pl.pallas_call(
        functools.partial(kernel, n, segs, kvh, slots, min(2, slots)),
        out_shape=pltpu.VMEM(queries.shape, jnp.bfloat16),
        in_specs=[scalars] * 2 + [anywhere] * 5,
        out_specs=pl.BlockSpec(memory_space=pltpu.VMEM),
        scratch_shapes=[
            pltpu.VMEM((kvh, tok, gw), jnp.bfloat16),
            pltpu.VMEM((kvh - 1, tok, gw), jnp.bfloat16),
            pltpu.VMEM(random_blocks.shape, jnp.int32),
            pltpu.VMEM(global_blocks.shape, jnp.int32),
            pltpu.SMEM(random_blocks.shape, jnp.int32),
            pltpu.SMEM(global_blocks.shape, jnp.int32),
            *[
                pltpu.VMEM((4 * chips * blk_dev, BLOCK, HEAD), jnp.bfloat16)
                for _ in range(slots + 1)
            ],
            pltpu.SemaphoreType.DMA((kvh,)),
            pltpu.SemaphoreType.DMA((slots + 1, 2)),
            pltpu.SemaphoreType.DMA((slots + 1, chips, 2)),
            pltpu.SemaphoreType.DMA((slots + 1, chips, 2)),
            pltpu.SemaphoreType.DMA((slots + 1,)),
            pltpu.SemaphoreType.DMA((slots + 1,)),
            pltpu.SemaphoreType.DMA((kvh,)),
            pltpu.SemaphoreType.DMA((kvh,)),
            pltpu.SemaphoreType.DMA((5,)),
            pltpu.SemaphoreType.DMA((5,)),
            pltpu.SemaphoreType.DMA((2,)),
            pltpu.SemaphoreType.REGULAR((slots,)),
            pltpu.SemaphoreType.REGULAR((slots,)),
        ],
        compiler_params=pltpu.CompilerParams(
            collective_id=0, has_side_effects=True, vmem_limit_bytes=46 * 1024 * 1024
        ),
        cost_estimate=pl.CostEstimate(
            flops=4 * tok * width * keys,
            bytes_accessed=4 * tok * width,
            transcendentals=tok * width // HEAD * keys,
        ),
    )(random_blocks, global_blocks, random_blocks, global_blocks, queries, keys_in, values_in)


def solution(mesh):
    in_specs = (
        P("segment", "seq", None),
        P("segment", "seq", None),
        P("segment", "seq", None),
        P("segment", "seq", None),
        P("segment", None),
    )
    out_specs = P("segment", "seq", None)
    return jax.shard_map(
        per_device, mesh=mesh, in_specs=in_specs, out_specs=out_specs, check_vma=False
    )
```

```python
import functools
import math

import jax
import jax.numpy as jnp
from jax import lax
from jax.experimental import pallas as pl
from jax.experimental.pallas import tpu as pltpu
from jax.sharding import PartitionSpec as P

HEAD = 128
BLOCK = 64
GLOB = 2
RAND = 3
MESH = pl.DeviceIdType.MESH
SLOT_BYTES = 16 * 1024 * 1024


def kernel(
    n, segs, kvh, slots, ahead,
    rand_ref, glob_ref, rand_hbm, glob_hbm, q_ref, k_ref, v_ref, out_ref,
    q_buf, res, rand_in, glob_in, rand_moved, glob_moved, *rest,
):
    kv = rest[: slots + 1]
    (
        q_sem, own_sem, send_sem, recv_sem, fsend, frecv,
        zsend, zrecv, ship_send, ship_recv, table_sem, free_c, free_p,
    ) = rest[slots + 1 :]
    tok = q_ref.shape[1]
    group = q_ref.shape[2] // (kvh * HEAD)
    gw = group * HEAD
    blk_dev = tok // BLOCK
    nblk = blk_dev * n
    chips = n // 2
    moved = kvh - 1
    me = lax.axis_index("seq")
    seg = lax.axis_index("segment")
    chip, core = me // 2, me % 2
    partner = chip * 2 + (1 - core)
    after, before = (seg + 1) % segs, (seg + segs - 1) % segs
    others = [(chip + o) % chips for o in range(1, chips)]

    def slot(h):
        return slots if h == moved else h % slots

    def q_copy(h):
        return pltpu.make_async_copy(
            q_ref.at[0, :, pl.ds(h * gw, gw)], q_buf.at[h], q_sem.at[h]
        )

    def place(s, c, i):
        return kv[s].at[pl.ds((core * 2 + i) * chips * blk_dev + c * blk_dev, blk_dev)]

    def own_rows(h, i):
        return (k_ref, v_ref)[i].at[:, :, pl.ds(h * HEAD, HEAD)]

    def own_copy(h, i):
        return pltpu.make_async_copy(
            own_rows(h, i), place(slot(h), chip, i), own_sem.at[slot(h), i]
        )

    def peer_copy(h, c, i):
        s = slot(h)
        return pltpu.make_async_remote_copy(
            src_ref=place(s, chip, i) if h == moved else own_rows(h, i),
            dst_ref=place(s, chip, i),
            send_sem=send_sem.at[s, c, i], recv_sem=recv_sem.at[s, chip, i],
            device_id={"seq": c * 2 + core}, device_id_type=MESH,
        )

    def peer_arrival(h, c, i):
        s = slot(h)
        return pltpu.make_async_remote_copy(
            src_ref=place(s, c, i), dst_ref=place(s, c, i),
            send_sem=send_sem.at[s, c, i], recv_sem=recv_sem.at[s, c, i],
            device_id={"seq": c * 2 + core}, device_id_type=MESH,
        )

    def forward(h, half):
        s = slot(h)
        part = kv[s].at[pl.ds(half * 2 * chips * blk_dev, 2 * chips * blk_dev)]
        return pltpu.make_async_remote_copy(
            src_ref=part, dst_ref=part,
            send_sem=fsend.at[s], recv_sem=frecv.at[s],
            device_id={"seq": partner}, device_id_type=MESH,
        )

    def ship(src, dst, k):
        return pltpu.make_async_remote_copy(
            src_ref=src, dst_ref=dst, send_sem=ship_send.at[k], recv_sem=ship_recv.at[k],
            device_id={"segment": after}, device_id_type=MESH,
        )

    shipped = [ship(own_rows(moved, i), place(slots, chip, i), i) for i in range(2)]
    shipped += [ship(rand_hbm, rand_in, 2), ship(glob_hbm, glob_in, 3)]
    shipped.append(ship(q_ref.at[0, :, pl.ds(moved * gw, gw)], q_buf.at[moved], 4))
    list_copies = [
        pltpu.make_async_copy(rand_in, rand_moved, table_sem.at[0]),
        pltpu.make_async_copy(glob_in, glob_moved, table_sem.at[1]),
    ]

    def start_gather(h):
        if slots <= h < moved:
            pl.semaphore_wait(free_c.at[h % slots], chips - 1)
        for i in range(2):
            if h == moved:
                shipped[i].wait_recv()
            for c in others:
                peer_copy(h, c, i).start()
            if h < moved:
                own_copy(h, i).start()

    barrier = pltpu.get_barrier_semaphore()
    greeted = [{"seq": c * 2 + core} for c in others]
    greeted += [{"seq": partner}, {"segment": after}, {"segment": before}]
    for who in greeted:
        pl.semaphore_signal(barrier, inc=1, device_id=who, device_id_type=MESH)
    q_copy(0).start()
    pl.semaphore_wait(barrier, len(greeted))

    for copy in shipped:
        copy.start()
    for h in range(ahead):
        start_gather(h)
    for h in range(1, moved):
        q_copy(h).start()

    scale = 1.0 / math.sqrt(HEAD)
    column = lax.broadcasted_iota(jnp.int32, (1, (3 + GLOB + RAND) * BLOCK), 1)

    for h in range(kvh):
        s = slot(h)
        for i in range(2):
            if h < moved:
                own_copy(h, i).wait()
            for c in others:
                peer_arrival(h, c, i).wait_recv()
        if slots <= h < moved:
            pl.semaphore_wait(free_p.at[s], 1)
        forward(h, core).start()
        if h + ahead < slots:
            start_gather(h + ahead)
        if h + ahead == moved:
            start_gather(moved)
        if h < moved:
            q_copy(h).wait()
        else:
            for arrival, copy in zip(shipped[2:4], list_copies):
                arrival.wait_recv()
                copy.start()
            for copy in list_copies:
                copy.wait()
            shipped[4].wait_recv()
        forward(h, 1 - core).wait_recv()

        def block_step(j, carry, h=h, s=s):
            rand, glob = (rand_ref, glob_ref) if h < moved else (rand_moved, glob_moved)
            row = me * blk_dev + j
            listed = [jnp.maximum(row - 1, 0), row, jnp.minimum(row + 1, nblk - 1)]
            listed += [glob[0, i] for i in range(GLOB)] + [rand[i, 0, j] for i in range(RAND)]

            def picked(i):
                parts = []
                for b in listed:
                    dev = lax.div(b, blk_dev)
                    where = (lax.rem(dev, 2) * 2 + i) * chips + lax.div(dev, 2)
                    parts.append(kv[s][where * blk_dev + lax.rem(b, blk_dev)])
                return jnp.concatenate(parts, axis=0)

            rows = pl.ds(pl.multiple_of(j * BLOCK, BLOCK), BLOCK)
            q_rows = q_buf[h, rows, :]
            q = jnp.concatenate([q_rows[:, g * HEAD : (g + 1) * HEAD] for g in range(group)], axis=0)
            scores = lax.dot_general(
                q, picked(0), (((1,), (1,)), ((), ())), preferred_element_type=jnp.float32
            )
            listed_here = ((column >= BLOCK) | (row >= 1)) & (
                (column < 2 * BLOCK) | (column >= 3 * BLOCK) | (row + 1 < nblk)
            )
            scores = scores * scale + jnp.where(listed_here, 0.0, -jnp.inf)
            top = jnp.max(scores, axis=-1, keepdims=True)
            expo = jnp.exp(scores - top)
            weights = (expo * (1.0 / jnp.sum(expo, axis=-1, keepdims=True))).astype(jnp.bfloat16)
            result = jnp.dot(weights, picked(1), preferred_element_type=jnp.float32)
            result = result.astype(jnp.bfloat16)
            for g in range(group):
                piece = result[g * BLOCK : (g + 1) * BLOCK, :]
                if h < moved:
                    res[h, rows, pl.ds(g * HEAD, HEAD)] = piece
                else:
                    out_ref[h, rows, pl.ds(g * HEAD, HEAD)] = piece
            if h < moved:
                pltpu.make_async_remote_copy(
                    src_ref=res.at[h, rows, :],
                    dst_ref=out_ref.at[h, rows, :],
                    send_sem=zsend.at[h], recv_sem=zrecv.at[h],
                    device_id={"segment": after}, device_id_type=MESH,
                ).start()
            return carry

        lax.fori_loop(0, blk_dev, block_step, 0)

        for i in range(2):
            for c in others:
                peer_copy(h, c, i).wait_send()
        forward(h, core).wait_send()
        if h + slots < moved:
            for c in others:
                pl.semaphore_signal(
                    free_c.at[s], inc=1, device_id={"seq": c * 2 + core}, device_id_type=MESH
                )
            pl.semaphore_signal(
                free_p.at[s], inc=1, device_id={"seq": partner}, device_id_type=MESH
            )
            start_gather(h + slots)

    for copy in shipped:
        copy.wait_send()
    for h in range(moved):
        pltpu.make_async_remote_copy(
            src_ref=res.at[h],
            dst_ref=out_ref.at[h],
            send_sem=zsend.at[h], recv_sem=zrecv.at[h],
            device_id={"segment": after}, device_id_type=MESH,
        ).wait()


def write_out(x_ref, out_ref, sems):
    heads, _, gw = x_ref.shape
    copies = [
        pltpu.make_async_copy(x_ref.at[h], out_ref.at[0, :, pl.ds(h * gw, gw)], sems.at[h])
        for h in range(heads)
    ]
    for copy in copies:
        copy.start()
    for copy in copies:
        copy.wait()


def per_device(queries, keys_in, values_in, random_blocks, global_blocks):
    n, segs = lax.axis_size("seq"), lax.axis_size("segment")
    tok, width = queries.shape[1:]
    kvh = keys_in.shape[2] // HEAD
    gw = width // kvh
    chips = n // 2
    blk_dev = tok // BLOCK
    slots = min(kvh - 1, max(2, SLOT_BYTES // (4 * n * tok * HEAD)))
    anywhere = pl.BlockSpec(memory_space=pl.ANY)
    scalars = pl.BlockSpec(memory_space=pltpu.SMEM)
    keys = (3 + GLOB + RAND) * BLOCK
    keys_in, values_in = (x.reshape(blk_dev, BLOCK, kvh * HEAD) for x in (keys_in, values_in))
    random_blocks = jnp.transpose(random_blocks, (2, 0, 1))
    landed = pl.pallas_call(
        functools.partial(kernel, n, segs, kvh, slots, min(2, slots)),
        out_shape=pltpu.VMEM((kvh, tok, gw), jnp.bfloat16),
        in_specs=[scalars] * 2 + [anywhere] * 5,
        out_specs=pl.BlockSpec(memory_space=pltpu.VMEM),
        scratch_shapes=[
            pltpu.VMEM((kvh, tok, gw), jnp.bfloat16),
            pltpu.VMEM((kvh - 1, tok, gw), jnp.bfloat16),
            pltpu.VMEM(random_blocks.shape, jnp.int32),
            pltpu.VMEM(global_blocks.shape, jnp.int32),
            pltpu.SMEM(random_blocks.shape, jnp.int32),
            pltpu.SMEM(global_blocks.shape, jnp.int32),
            *[
                pltpu.VMEM((4 * chips * blk_dev, BLOCK, HEAD), jnp.bfloat16)
                for _ in range(slots + 1)
            ],
            pltpu.SemaphoreType.DMA((kvh,)),
            pltpu.SemaphoreType.DMA((slots + 1, 2)),
            pltpu.SemaphoreType.DMA((slots + 1, chips, 2)),
            pltpu.SemaphoreType.DMA((slots + 1, chips, 2)),
            pltpu.SemaphoreType.DMA((slots + 1,)),
            pltpu.SemaphoreType.DMA((slots + 1,)),
            pltpu.SemaphoreType.DMA((kvh,)),
            pltpu.SemaphoreType.DMA((kvh,)),
            pltpu.SemaphoreType.DMA((5,)),
            pltpu.SemaphoreType.DMA((5,)),
            pltpu.SemaphoreType.DMA((2,)),
            pltpu.SemaphoreType.REGULAR((slots,)),
            pltpu.SemaphoreType.REGULAR((slots,)),
        ],
        compiler_params=pltpu.CompilerParams(
            collective_id=0, has_side_effects=True, vmem_limit_bytes=46 * 1024 * 1024
        ),
        cost_estimate=pl.CostEstimate(
            flops=4 * tok * width * keys,
            bytes_accessed=4 * tok * width,
            transcendentals=tok * width // HEAD * keys,
        ),
    )(random_blocks, global_blocks, random_blocks, global_blocks, queries, keys_in, values_in)
    return pl.pallas_call(
        write_out,
        out_shape=jax.ShapeDtypeStruct(queries.shape, jnp.bfloat16),
        in_specs=[pl.BlockSpec(memory_space=pltpu.VMEM)],
        out_specs=anywhere,
        scratch_shapes=[pltpu.SemaphoreType.DMA((kvh,))],
        cost_estimate=pl.CostEstimate(
            flops=0, bytes_accessed=2 * tok * width, transcendentals=0
        ),
    )(landed)


def solution(mesh):
    in_specs = (
        P("segment", "seq", None),
        P("segment", "seq", None),
        P("segment", "seq", None),
        P("segment", "seq", None),
        P("segment", None),
    )
    out_specs = P("segment", "seq", None)
    return jax.shard_map(
        per_device, mesh=mesh, in_specs=in_specs, out_specs=out_specs, check_vma=False
    )
```

```python
import functools
import math

import jax
import jax.numpy as jnp
from jax import lax
from jax.experimental import pallas as pl
from jax.experimental.pallas import tpu as pltpu
from jax.sharding import PartitionSpec as P

HEAD = 128
BLOCK = 64
GLOB = 2
RAND = 3
MESH = pl.DeviceIdType.MESH
SLOT_BYTES = 16 * 1024 * 1024


def kernel(
    n, segs, kvh, slots, ahead,
    rand_ref, glob_ref, rand_hbm, glob_hbm, q_ref, k_ref, v_ref, out_ref,
    q_buf, res, rand_in, glob_in, rand_moved, glob_moved, *rest,
):
    kv = rest[: slots + 1]
    (
        q_sem, own_sem, send_sem, recv_sem, fsend, frecv,
        zsend, zrecv, ship_send, ship_recv, table_sem, free_c, free_p,
    ) = rest[slots + 1 :]
    tok = q_ref.shape[1]
    group = q_ref.shape[2] // (kvh * HEAD)
    gw = group * HEAD
    blk_dev = tok // BLOCK
    nblk = blk_dev * n
    chips = n // 2
    moved = kvh - 1
    me = lax.axis_index("seq")
    seg = lax.axis_index("segment")
    chip, core = me // 2, me % 2
    partner = chip * 2 + (1 - core)
    after, before = (seg + 1) % segs, (seg + segs - 1) % segs
    others = [(chip + o) % chips for o in range(1, chips)]

    def slot(h):
        return slots if h == moved else h % slots

    def q_copy(h):
        return pltpu.make_async_copy(
            q_ref.at[0, :, pl.ds(h * gw, gw)], q_buf.at[h], q_sem.at[h]
        )

    def place(s, c, i):
        return kv[s].at[pl.ds((core * 2 + i) * chips * blk_dev + c * blk_dev, blk_dev)]

    def own_rows(h, i):
        return (k_ref, v_ref)[i].at[:, :, pl.ds(h * HEAD, HEAD)]

    def own_copy(h, i):
        return pltpu.make_async_copy(
            own_rows(h, i), place(slot(h), chip, i), own_sem.at[slot(h), i]
        )

    def peer_copy(h, c, i):
        s = slot(h)
        return pltpu.make_async_remote_copy(
            src_ref=place(s, chip, i) if h == moved else own_rows(h, i),
            dst_ref=place(s, chip, i),
            send_sem=send_sem.at[s, c, i], recv_sem=recv_sem.at[s, chip, i],
            device_id={"seq": c * 2 + core}, device_id_type=MESH,
        )

    def peer_arrival(h, c, i):
        s = slot(h)
        return pltpu.make_async_remote_copy(
            src_ref=place(s, c, i), dst_ref=place(s, c, i),
            send_sem=send_sem.at[s, c, i], recv_sem=recv_sem.at[s, c, i],
            device_id={"seq": c * 2 + core}, device_id_type=MESH,
        )

    def forward(h, half):
        s = slot(h)
        part = kv[s].at[pl.ds(half * 2 * chips * blk_dev, 2 * chips * blk_dev)]
        return pltpu.make_async_remote_copy(
            src_ref=part, dst_ref=part,
            send_sem=fsend.at[s], recv_sem=frecv.at[s],
            device_id={"seq": partner}, device_id_type=MESH,
        )

    def ship(src, dst, k):
        return pltpu.make_async_remote_copy(
            src_ref=src, dst_ref=dst, send_sem=ship_send.at[k], recv_sem=ship_recv.at[k],
            device_id={"segment": after}, device_id_type=MESH,
        )

    shipped = [ship(own_rows(moved, i), place(slots, chip, i), i) for i in range(2)]
    shipped += [ship(rand_hbm, rand_in, 2), ship(glob_hbm, glob_in, 3)]
    shipped.append(ship(q_ref.at[0, :, pl.ds(moved * gw, gw)], q_buf.at[moved], 4))
    list_copies = [
        pltpu.make_async_copy(rand_in, rand_moved, table_sem.at[0]),
        pltpu.make_async_copy(glob_in, glob_moved, table_sem.at[1]),
    ]

    def hand_over(h, part, pieces):
        rows = pl.ds(part * tok // pieces, tok // pieces)
        return pltpu.make_async_remote_copy(
            src_ref=res.at[h, rows, :],
            dst_ref=out_ref.at[0, rows, pl.ds(h * gw, gw)],
            send_sem=zsend.at[h], recv_sem=zrecv.at[h],
            device_id={"segment": after}, device_id_type=MESH,
        )

    def start_gather(h):
        if slots <= h < moved:
            pl.semaphore_wait(free_c.at[h % slots], chips - 1)
        for i in range(2):
            if h == moved:
                shipped[i].wait_recv()
            for c in others:
                peer_copy(h, c, i).start()
            if h < moved:
                own_copy(h, i).start()

    barrier = pltpu.get_barrier_semaphore()
    greeted = [{"seq": c * 2 + core} for c in others]
    greeted += [{"seq": partner}, {"segment": after}, {"segment": before}]
    for who in greeted:
        pl.semaphore_signal(barrier, inc=1, device_id=who, device_id_type=MESH)
    q_copy(0).start()
    pl.semaphore_wait(barrier, len(greeted))

    for copy in shipped:
        copy.start()
    for h in range(ahead):
        start_gather(h)
    for h in range(1, moved):
        q_copy(h).start()

    scale = 1.0 / math.sqrt(HEAD)
    column = lax.broadcasted_iota(jnp.int32, (1, (3 + GLOB + RAND) * BLOCK), 1)

    for h in range(kvh):
        s = slot(h)
        for i in range(2):
            if h < moved:
                own_copy(h, i).wait()
            for c in others:
                peer_arrival(h, c, i).wait_recv()
        if slots <= h < moved:
            pl.semaphore_wait(free_p.at[s], 1)
        forward(h, core).start()
        if h + ahead < slots:
            start_gather(h + ahead)
        if h + ahead == moved:
            start_gather(moved)
        if h < moved:
            q_copy(h).wait()
        else:
            for arrival, copy in zip(shipped[2:4], list_copies):
                arrival.wait_recv()
                copy.start()
            for copy in list_copies:
                copy.wait()
            shipped[4].wait_recv()
        forward(h, 1 - core).wait_recv()

        def block_step(j, carry, h=h, s=s):
            rand, glob = (rand_ref, glob_ref) if h < moved else (rand_moved, glob_moved)
            row = me * blk_dev + j
            listed = [jnp.maximum(row - 1, 0), row, jnp.minimum(row + 1, nblk - 1)]
            listed += [glob[0, i] for i in range(GLOB)] + [rand[i, 0, j] for i in range(RAND)]

            def picked(i):
                parts = []
                for b in listed:
                    dev = lax.div(b, blk_dev)
                    where = (lax.rem(dev, 2) * 2 + i) * chips + lax.div(dev, 2)
                    parts.append(kv[s][where * blk_dev + lax.rem(b, blk_dev)])
                return jnp.concatenate(parts, axis=0)

            rows = pl.ds(pl.multiple_of(j * BLOCK, BLOCK), BLOCK)
            q_rows = q_buf[h, rows, :]
            q = jnp.concatenate([q_rows[:, g * HEAD : (g + 1) * HEAD] for g in range(group)], axis=0)
            scores = lax.dot_general(
                q, picked(0), (((1,), (1,)), ((), ())), preferred_element_type=jnp.float32
            )
            listed_here = ((column >= BLOCK) | (row >= 1)) & (
                (column < 2 * BLOCK) | (column >= 3 * BLOCK) | (row + 1 < nblk)
            )
            scores = scores * scale + jnp.where(listed_here, 0.0, -jnp.inf)
            top = jnp.max(scores, axis=-1, keepdims=True)
            expo = jnp.exp(scores - top)
            weights = (expo * (1.0 / jnp.sum(expo, axis=-1, keepdims=True))).astype(jnp.bfloat16)
            result = jnp.dot(weights, picked(1), preferred_element_type=jnp.float32)
            result = result.astype(jnp.bfloat16)
            for g in range(group):
                piece = result[g * BLOCK : (g + 1) * BLOCK, :]
                if h < moved:
                    res[h, rows, pl.ds(g * HEAD, HEAD)] = piece
                else:
                    out_ref[0, rows, pl.ds(h * gw + g * HEAD, HEAD)] = piece
            return carry

        pieces = 2 if h == 0 else 1
        for part in range(pieces):
            lax.fori_loop(
                part * blk_dev // pieces, (part + 1) * blk_dev // pieces, block_step, 0
            )
            if h < moved:
                hand_over(h, part, pieces).start()

        for i in range(2):
            for c in others:
                peer_copy(h, c, i).wait_send()
        forward(h, core).wait_send()
        if h + slots < moved:
            for c in others:
                pl.semaphore_signal(
                    free_c.at[s], inc=1, device_id={"seq": c * 2 + core}, device_id_type=MESH
                )
            pl.semaphore_signal(
                free_p.at[s], inc=1, device_id={"seq": partner}, device_id_type=MESH
            )
            start_gather(h + slots)

    for copy in shipped:
        copy.wait_send()
    for h in range(moved):
        hand_over(h, 0, 1).wait()


def per_device(queries, keys_in, values_in, random_blocks, global_blocks):
    n, segs = lax.axis_size("seq"), lax.axis_size("segment")
    tok, width = queries.shape[1:]
    kvh = keys_in.shape[2] // HEAD
    gw = width // kvh
    chips = n // 2
    blk_dev = tok // BLOCK
    slots = min(kvh - 1, max(2, SLOT_BYTES // (4 * n * tok * HEAD)))
    anywhere = pl.BlockSpec(memory_space=pl.ANY)
    scalars = pl.BlockSpec(memory_space=pltpu.SMEM)
    keys = (3 + GLOB + RAND) * BLOCK
    keys_in, values_in = (x.reshape(blk_dev, BLOCK, kvh * HEAD) for x in (keys_in, values_in))
    random_blocks = jnp.transpose(random_blocks, (2, 0, 1))
    return pl.pallas_call(
        functools.partial(kernel, n, segs, kvh, slots, min(2, slots)),
        out_shape=pltpu.VMEM(queries.shape, jnp.bfloat16),
        in_specs=[scalars] * 2 + [anywhere] * 5,
        out_specs=pl.BlockSpec(memory_space=pltpu.VMEM),
        scratch_shapes=[
            pltpu.VMEM((kvh, tok, gw), jnp.bfloat16),
            pltpu.VMEM((kvh - 1, tok, gw), jnp.bfloat16),
            pltpu.VMEM(random_blocks.shape, jnp.int32),
            pltpu.VMEM(global_blocks.shape, jnp.int32),
            pltpu.SMEM(random_blocks.shape, jnp.int32),
            pltpu.SMEM(global_blocks.shape, jnp.int32),
            *[
                pltpu.VMEM((4 * chips * blk_dev, BLOCK, HEAD), jnp.bfloat16)
                for _ in range(slots + 1)
            ],
            pltpu.SemaphoreType.DMA((kvh,)),
            pltpu.SemaphoreType.DMA((slots + 1, 2)),
            pltpu.SemaphoreType.DMA((slots + 1, chips, 2)),
            pltpu.SemaphoreType.DMA((slots + 1, chips, 2)),
            pltpu.SemaphoreType.DMA((slots + 1,)),
            pltpu.SemaphoreType.DMA((slots + 1,)),
            pltpu.SemaphoreType.DMA((kvh,)),
            pltpu.SemaphoreType.DMA((kvh,)),
            pltpu.SemaphoreType.DMA((5,)),
            pltpu.SemaphoreType.DMA((5,)),
            pltpu.SemaphoreType.DMA((2,)),
            pltpu.SemaphoreType.REGULAR((slots,)),
            pltpu.SemaphoreType.REGULAR((slots,)),
        ],
        compiler_params=pltpu.CompilerParams(
            collective_id=0, has_side_effects=True, vmem_limit_bytes=46 * 1024 * 1024
        ),
        cost_estimate=pl.CostEstimate(
            flops=4 * tok * width * keys,
            bytes_accessed=4 * tok * width,
            transcendentals=tok * width // HEAD * keys,
        ),
    )(random_blocks, global_blocks, random_blocks, global_blocks, queries, keys_in, values_in)


def solution(mesh):
    in_specs = (
        P("segment", "seq", None),
        P("segment", "seq", None),
        P("segment", "seq", None),
        P("segment", "seq", None),
        P("segment", None),
    )
    out_specs = P("segment", "seq", None)
    return jax.shard_map(
        per_device, mesh=mesh, in_specs=in_specs, out_specs=out_specs, check_vma=False
    )
```

```python
import functools
import math

import jax
import jax.numpy as jnp
from jax import lax
from jax.experimental import pallas as pl
from jax.experimental.pallas import tpu as pltpu
from jax.sharding import PartitionSpec as P

HEAD = 128
BLOCK = 64
GLOB = 2
RAND = 3
MESH = pl.DeviceIdType.MESH
PIECES = 8
SLOT_BYTES = 16 * 1024 * 1024


def kernel(
    n, segs, kvh, slots, ahead,
    rand_ref, glob_ref, rand_hbm, glob_hbm, q_ref, k_ref, v_ref, out_ref,
    q_buf, res, rand_in, glob_in, rand_moved, glob_moved, *rest,
):
    kv = rest[: slots + 1]
    (
        q_sem, own_sem, send_sem, recv_sem, fsend, frecv,
        zsend, zrecv, ship_send, ship_recv, table_sem, free_c, free_p,
    ) = rest[slots + 1 :]
    tok = q_ref.shape[1]
    group = q_ref.shape[2] // (kvh * HEAD)
    gw = group * HEAD
    blk_dev = tok // BLOCK
    nblk = blk_dev * n
    chips = n // 2
    moved = kvh - 1
    me = lax.axis_index("seq")
    seg = lax.axis_index("segment")
    chip, core = me // 2, me % 2
    partner = chip * 2 + (1 - core)
    after, before = (seg + 1) % segs, (seg + segs - 1) % segs
    others = [(chip + o) % chips for o in range(1, chips)]

    def slot(h):
        return slots if h == moved else h % slots

    def q_copy(h):
        return pltpu.make_async_copy(
            q_ref.at[0, :, pl.ds(h * gw, gw)], q_buf.at[h], q_sem.at[h]
        )

    def place(s, c, i):
        return kv[s].at[pl.ds((core * 2 + i) * chips * blk_dev + c * blk_dev, blk_dev)]

    def own_rows(h, i):
        return (k_ref, v_ref)[i].at[:, :, pl.ds(h * HEAD, HEAD)]

    def own_copy(h, i):
        return pltpu.make_async_copy(
            own_rows(h, i), place(slot(h), chip, i), own_sem.at[slot(h), i]
        )

    def peer_copy(h, c, i):
        s = slot(h)
        return pltpu.make_async_remote_copy(
            src_ref=place(s, chip, i) if h == moved else own_rows(h, i),
            dst_ref=place(s, chip, i),
            send_sem=send_sem.at[s, c, i], recv_sem=recv_sem.at[s, chip, i],
            device_id={"seq": c * 2 + core}, device_id_type=MESH,
        )

    def peer_arrival(h, c, i):
        s = slot(h)
        return pltpu.make_async_remote_copy(
            src_ref=place(s, c, i), dst_ref=place(s, c, i),
            send_sem=send_sem.at[s, c, i], recv_sem=recv_sem.at[s, c, i],
            device_id={"seq": c * 2 + core}, device_id_type=MESH,
        )

    def forward(h, half):
        s = slot(h)
        part = kv[s].at[pl.ds(half * 2 * chips * blk_dev, 2 * chips * blk_dev)]
        return pltpu.make_async_remote_copy(
            src_ref=part, dst_ref=part,
            send_sem=fsend.at[s], recv_sem=frecv.at[s],
            device_id={"seq": partner}, device_id_type=MESH,
        )

    def ship(src, dst, k):
        return pltpu.make_async_remote_copy(
            src_ref=src, dst_ref=dst, send_sem=ship_send.at[k], recv_sem=ship_recv.at[k],
            device_id={"segment": after}, device_id_type=MESH,
        )

    shipped = [ship(own_rows(moved, i), place(slots, chip, i), i) for i in range(2)]
    shipped += [ship(rand_hbm, rand_in, 2), ship(glob_hbm, glob_in, 3)]
    shipped.append(ship(q_ref.at[0, :, pl.ds(moved * gw, gw)], q_buf.at[moved], 4))
    list_copies = [
        pltpu.make_async_copy(rand_in, rand_moved, table_sem.at[0]),
        pltpu.make_async_copy(glob_in, glob_moved, table_sem.at[1]),
    ]

    def hand_over(h, part, pieces):
        rows = pl.ds(part * tok // pieces, tok // pieces)
        return pltpu.make_async_remote_copy(
            src_ref=res.at[h, rows, :],
            dst_ref=out_ref.at[0, rows, pl.ds(h * gw, gw)],
            send_sem=zsend.at[h], recv_sem=zrecv.at[h],
            device_id={"segment": after}, device_id_type=MESH,
        )

    def start_gather(h):
        if slots <= h < moved:
            pl.semaphore_wait(free_c.at[h % slots], chips - 1)
        for i in range(2):
            if h == moved:
                shipped[i].wait_recv()
            for c in others:
                peer_copy(h, c, i).start()
            if h < moved:
                own_copy(h, i).start()

    barrier = pltpu.get_barrier_semaphore()
    greeted = [{"seq": c * 2 + core} for c in others]
    greeted += [{"seq": partner}, {"segment": after}, {"segment": before}]
    for who in greeted:
        pl.semaphore_signal(barrier, inc=1, device_id=who, device_id_type=MESH)
    q_copy(0).start()
    pl.semaphore_wait(barrier, len(greeted))

    for copy in shipped:
        copy.start()
    for h in range(ahead):
        start_gather(h)
    for h in range(1, moved):
        q_copy(h).start()

    scale = 1.0 / math.sqrt(HEAD)
    column = lax.broadcasted_iota(jnp.int32, (1, (3 + GLOB + RAND) * BLOCK), 1)

    for h in range(kvh):
        s = slot(h)
        for i in range(2):
            if h < moved:
                own_copy(h, i).wait()
            for c in others:
                peer_arrival(h, c, i).wait_recv()
        if slots <= h < moved:
            pl.semaphore_wait(free_p.at[s], 1)
        forward(h, core).start()
        if h + ahead < slots:
            start_gather(h + ahead)
        if h + ahead == moved:
            start_gather(moved)
        if h < moved:
            q_copy(h).wait()
        else:
            for arrival, copy in zip(shipped[2:4], list_copies):
                arrival.wait_recv()
                copy.start()
            for copy in list_copies:
                copy.wait()
            shipped[4].wait_recv()
        forward(h, 1 - core).wait_recv()

        def block_step(j, carry, h=h, s=s):
            rand, glob = (rand_ref, glob_ref) if h < moved else (rand_moved, glob_moved)
            row = me * blk_dev + j
            listed = [jnp.maximum(row - 1, 0), row, jnp.minimum(row + 1, nblk - 1)]
            listed += [glob[0, i] for i in range(GLOB)] + [rand[i, 0, j] for i in range(RAND)]

            def picked(i):
                parts = []
                for b in listed:
                    dev = lax.div(b, blk_dev)
                    where = (lax.rem(dev, 2) * 2 + i) * chips + lax.div(dev, 2)
                    parts.append(kv[s][where * blk_dev + lax.rem(b, blk_dev)])
                return jnp.concatenate(parts, axis=0)

            rows = pl.ds(pl.multiple_of(j * BLOCK, BLOCK), BLOCK)
            q_rows = q_buf[h, rows, :]
            q = jnp.concatenate([q_rows[:, g * HEAD : (g + 1) * HEAD] for g in range(group)], axis=0)
            scores = lax.dot_general(
                q, picked(0), (((1,), (1,)), ((), ())), preferred_element_type=jnp.float32
            )
            listed_here = ((column >= BLOCK) | (row >= 1)) & (
                (column < 2 * BLOCK) | (column >= 3 * BLOCK) | (row + 1 < nblk)
            )
            scores = scores * scale + jnp.where(listed_here, 0.0, -jnp.inf)
            top = jnp.max(scores, axis=-1, keepdims=True)
            expo = jnp.exp(scores - top)
            weights = (expo * (1.0 / jnp.sum(expo, axis=-1, keepdims=True))).astype(jnp.bfloat16)
            result = jnp.dot(weights, picked(1), preferred_element_type=jnp.float32)
            result = result.astype(jnp.bfloat16)
            for g in range(group):
                piece = result[g * BLOCK : (g + 1) * BLOCK, :]
                if h < moved:
                    res[h, rows, pl.ds(g * HEAD, HEAD)] = piece
                else:
                    out_ref[0, rows, pl.ds(h * gw + g * HEAD, HEAD)] = piece
            return carry

        pieces = 2 if h == 0 else 1
        for part in range(pieces):
            lax.fori_loop(
                part * blk_dev // pieces, (part + 1) * blk_dev // pieces, block_step, 0
            )
            if h < moved:
                hand_over(h, part, pieces).start()

        for i in range(2):
            for c in others:
                peer_copy(h, c, i).wait_send()
        forward(h, core).wait_send()
        if h + slots < moved:
            for c in others:
                pl.semaphore_signal(
                    free_c.at[s], inc=1, device_id={"seq": c * 2 + core}, device_id_type=MESH
                )
            pl.semaphore_signal(
                free_p.at[s], inc=1, device_id={"seq": partner}, device_id_type=MESH
            )
            start_gather(h + slots)

    for copy in shipped:
        copy.wait_send()
    for h in range(moved):
        hand_over(h, 0, 1).wait()


def write_out(x_ref, out_ref, sems):
    rows = out_ref.shape[1] // PIECES
    copies = [
        pltpu.make_async_copy(
            x_ref.at[:, pl.ds(i * rows, rows), :], out_ref.at[:, pl.ds(i * rows, rows), :], sems.at[i]
        )
        for i in range(PIECES)
    ]
    for copy in copies:
        copy.start()
    for copy in copies:
        copy.wait()


def per_device(queries, keys_in, values_in, random_blocks, global_blocks):
    n, segs = lax.axis_size("seq"), lax.axis_size("segment")
    tok, width = queries.shape[1:]
    kvh = keys_in.shape[2] // HEAD
    gw = width // kvh
    chips = n // 2
    blk_dev = tok // BLOCK
    slots = min(kvh - 1, max(2, SLOT_BYTES // (4 * n * tok * HEAD)))
    anywhere = pl.BlockSpec(memory_space=pl.ANY)
    scalars = pl.BlockSpec(memory_space=pltpu.SMEM)
    keys = (3 + GLOB + RAND) * BLOCK
    keys_in, values_in = (x.reshape(blk_dev, BLOCK, kvh * HEAD) for x in (keys_in, values_in))
    random_blocks = jnp.transpose(random_blocks, (2, 0, 1))
    landed = pl.pallas_call(
        functools.partial(kernel, n, segs, kvh, slots, min(2, slots)),
        out_shape=pltpu.VMEM(queries.shape, jnp.bfloat16),
        in_specs=[scalars] * 2 + [anywhere] * 5,
        out_specs=pl.BlockSpec(memory_space=pltpu.VMEM),
        scratch_shapes=[
            pltpu.VMEM((kvh, tok, gw), jnp.bfloat16),
            pltpu.VMEM((kvh - 1, tok, gw), jnp.bfloat16),
            pltpu.VMEM(random_blocks.shape, jnp.int32),
            pltpu.VMEM(global_blocks.shape, jnp.int32),
            pltpu.SMEM(random_blocks.shape, jnp.int32),
            pltpu.SMEM(global_blocks.shape, jnp.int32),
            *[
                pltpu.VMEM((4 * chips * blk_dev, BLOCK, HEAD), jnp.bfloat16)
                for _ in range(slots + 1)
            ],
            pltpu.SemaphoreType.DMA((kvh,)),
            pltpu.SemaphoreType.DMA((slots + 1, 2)),
            pltpu.SemaphoreType.DMA((slots + 1, chips, 2)),
            pltpu.SemaphoreType.DMA((slots + 1, chips, 2)),
            pltpu.SemaphoreType.DMA((slots + 1,)),
            pltpu.SemaphoreType.DMA((slots + 1,)),
            pltpu.SemaphoreType.DMA((kvh,)),
            pltpu.SemaphoreType.DMA((kvh,)),
            pltpu.SemaphoreType.DMA((5,)),
            pltpu.SemaphoreType.DMA((5,)),
            pltpu.SemaphoreType.DMA((2,)),
            pltpu.SemaphoreType.REGULAR((slots,)),
            pltpu.SemaphoreType.REGULAR((slots,)),
        ],
        compiler_params=pltpu.CompilerParams(
            collective_id=0, has_side_effects=True, vmem_limit_bytes=46 * 1024 * 1024
        ),
        cost_estimate=pl.CostEstimate(
            flops=4 * tok * width * keys,
            bytes_accessed=4 * tok * width,
            transcendentals=tok * width // HEAD * keys,
        ),
    )(random_blocks, global_blocks, random_blocks, global_blocks, queries, keys_in, values_in)
    return pl.pallas_call(
        write_out,
        out_shape=pltpu.HBM(queries.shape, jnp.bfloat16),
        in_specs=[pl.BlockSpec(memory_space=pltpu.VMEM)],
        out_specs=pl.BlockSpec(memory_space=pltpu.HBM),
        scratch_shapes=[pltpu.SemaphoreType.DMA((PIECES,))],
        cost_estimate=pl.CostEstimate(
            flops=0, bytes_accessed=2 * tok * width, transcendentals=0
        ),
    )(landed)


def solution(mesh):
    in_specs = (
        P("segment", "seq", None),
        P("segment", "seq", None),
        P("segment", "seq", None),
        P("segment", "seq", None),
        P("segment", None),
    )
    out_specs = P("segment", "seq", None)
    return jax.shard_map(
        per_device, mesh=mesh, in_specs=in_specs, out_specs=out_specs, check_vma=False
    )
```

```python
import functools
import math

import jax
import jax.numpy as jnp
from jax import lax
from jax.experimental import pallas as pl
from jax.experimental.pallas import tpu as pltpu
from jax.sharding import PartitionSpec as P

HEAD = 128
BLOCK = 64
GLOB = 2
RAND = 3
MESH = pl.DeviceIdType.MESH
PIECES = 8
SLOT_BYTES = 16 * 1024 * 1024


def kernel(
    n, segs, kvh, slots, ahead,
    rand_ref, glob_ref, rand_hbm, glob_hbm, q_ref, k_ref, v_ref, out_ref,
    q_buf, res, rand_in, glob_in, rand_moved, glob_moved, *rest,
):
    kv = rest[: slots + 1]
    (
        q_sem, own_sem, send_sem, recv_sem, fsend, frecv,
        zsend, zrecv, ship_send, ship_recv, table_sem, free_c, free_p,
    ) = rest[slots + 1 :]
    tok = q_ref.shape[1]
    group = q_ref.shape[2] // (kvh * HEAD)
    gw = group * HEAD
    blk_dev = tok // BLOCK
    nblk = blk_dev * n
    chips = n // 2
    moved = kvh - 1
    me = lax.axis_index("seq")
    seg = lax.axis_index("segment")
    chip, core = me // 2, me % 2
    partner = chip * 2 + (1 - core)
    after, before = (seg + 1) % segs, (seg + segs - 1) % segs
    others = [(chip + o) % chips for o in range(1, chips)]

    def slot(h):
        return slots if h == moved else h % slots

    def q_copy(h):
        return pltpu.make_async_copy(
            q_ref.at[0, :, pl.ds(h * gw, gw)], q_buf.at[h], q_sem.at[h]
        )

    def place(s, c, i):
        return kv[s].at[pl.ds((core * 2 + i) * chips * blk_dev + c * blk_dev, blk_dev)]

    def own_rows(h, i):
        return (k_ref, v_ref)[i].at[:, :, pl.ds(h * HEAD, HEAD)]

    def own_copy(h, i):
        return pltpu.make_async_copy(
            own_rows(h, i), place(slot(h), chip, i), own_sem.at[slot(h), i]
        )

    def peer_copy(h, c, i):
        s = slot(h)
        return pltpu.make_async_remote_copy(
            src_ref=place(s, chip, i) if h == moved else own_rows(h, i),
            dst_ref=place(s, chip, i),
            send_sem=send_sem.at[s, c, i], recv_sem=recv_sem.at[s, chip, i],
            device_id={"seq": c * 2 + core}, device_id_type=MESH,
        )

    def peer_arrival(h, c, i):
        s = slot(h)
        return pltpu.make_async_remote_copy(
            src_ref=place(s, c, i), dst_ref=place(s, c, i),
            send_sem=send_sem.at[s, c, i], recv_sem=recv_sem.at[s, c, i],
            device_id={"seq": c * 2 + core}, device_id_type=MESH,
        )

    def forward(h, half):
        s = slot(h)
        part = kv[s].at[pl.ds(half * 2 * chips * blk_dev, 2 * chips * blk_dev)]
        return pltpu.make_async_remote_copy(
            src_ref=part, dst_ref=part,
            send_sem=fsend.at[s], recv_sem=frecv.at[s],
            device_id={"seq": partner}, device_id_type=MESH,
        )

    def ship(src, dst, k):
        return pltpu.make_async_remote_copy(
            src_ref=src, dst_ref=dst, send_sem=ship_send.at[k], recv_sem=ship_recv.at[k],
            device_id={"segment": after}, device_id_type=MESH,
        )

    shipped = [ship(own_rows(moved, i), place(slots, chip, i), i) for i in range(2)]
    shipped += [ship(rand_hbm, rand_in, 2), ship(glob_hbm, glob_in, 3)]
    shipped.append(ship(q_ref.at[0, :, pl.ds(moved * gw, gw)], q_buf.at[moved], 4))
    list_copies = [
        pltpu.make_async_copy(rand_in, rand_moved, table_sem.at[0]),
        pltpu.make_async_copy(glob_in, glob_moved, table_sem.at[1]),
    ]

    def hand_over(h, part, pieces):
        rows = pl.ds(part * tok // pieces, tok // pieces)
        return pltpu.make_async_remote_copy(
            src_ref=res.at[h, rows, :],
            dst_ref=out_ref.at[0, rows, pl.ds(h * gw, gw)],
            send_sem=zsend.at[h], recv_sem=zrecv.at[h],
            device_id={"segment": after}, device_id_type=MESH,
        )

    def start_gather(h):
        if slots <= h < moved:
            pl.semaphore_wait(free_c.at[h % slots], chips - 1)
        for i in range(2):
            if h == moved:
                shipped[i].wait_recv()
            for c in others:
                peer_copy(h, c, i).start()
            if h < moved:
                own_copy(h, i).start()

    barrier = pltpu.get_barrier_semaphore()
    greeted = [{"seq": c * 2 + core} for c in others]
    greeted += [{"seq": partner}, {"segment": after}, {"segment": before}]
    for who in greeted:
        pl.semaphore_signal(barrier, inc=1, device_id=who, device_id_type=MESH)
    q_copy(0).start()
    pl.semaphore_wait(barrier, len(greeted))

    for copy in shipped:
        copy.start()
    for h in range(ahead):
        start_gather(h)
    for h in range(1, moved):
        q_copy(h).start()

    scale = 1.0 / math.sqrt(HEAD)
    column = lax.broadcasted_iota(jnp.int32, (1, (3 + GLOB + RAND) * BLOCK), 1)

    for h in range(kvh):
        s = slot(h)
        for i in range(2):
            if h < moved:
                own_copy(h, i).wait()
            for c in others:
                peer_arrival(h, c, i).wait_recv()
        if slots <= h < moved:
            pl.semaphore_wait(free_p.at[s], 1)
        forward(h, core).start()
        if h + ahead < slots:
            start_gather(h + ahead)
        if h + ahead == moved:
            start_gather(moved)
        if h < moved:
            q_copy(h).wait()
        else:
            for arrival, copy in zip(shipped[2:4], list_copies):
                arrival.wait_recv()
                copy.start()
            for copy in list_copies:
                copy.wait()
            shipped[4].wait_recv()
        forward(h, 1 - core).wait_recv()

        def block_step(j, carry, h=h, s=s):
            rand, glob = (rand_ref, glob_ref) if h < moved else (rand_moved, glob_moved)
            row = me * blk_dev + j
            listed = [jnp.maximum(row - 1, 0), row, jnp.minimum(row + 1, nblk - 1)]
            listed += [glob[0, i] for i in range(GLOB)] + [rand[i, 0, j] for i in range(RAND)]

            def picked(i):
                parts = []
                for b in listed:
                    dev = lax.div(b, blk_dev)
                    where = (lax.rem(dev, 2) * 2 + i) * chips + lax.div(dev, 2)
                    parts.append(kv[s][where * blk_dev + lax.rem(b, blk_dev)])
                return jnp.concatenate(parts, axis=0)

            rows = pl.ds(pl.multiple_of(j * BLOCK, BLOCK), BLOCK)
            q_rows = q_buf[h, rows, :]
            q = jnp.concatenate([q_rows[:, g * HEAD : (g + 1) * HEAD] for g in range(group)], axis=0)
            scores = lax.dot_general(
                q, picked(0), (((1,), (1,)), ((), ())), preferred_element_type=jnp.float32
            )
            listed_here = ((column >= BLOCK) | (row >= 1)) & (
                (column < 2 * BLOCK) | (column >= 3 * BLOCK) | (row + 1 < nblk)
            )
            scores = scores * scale + jnp.where(listed_here, 0.0, -jnp.inf)
            top = jnp.max(scores, axis=-1, keepdims=True)
            expo = jnp.exp(scores - top)
            weights = (expo * (1.0 / jnp.sum(expo, axis=-1, keepdims=True))).astype(jnp.bfloat16)
            result = jnp.dot(weights, picked(1), preferred_element_type=jnp.float32)
            result = result.astype(jnp.bfloat16)
            for g in range(group):
                piece = result[g * BLOCK : (g + 1) * BLOCK, :]
                if h < moved:
                    res[h, rows, pl.ds(g * HEAD, HEAD)] = piece
                else:
                    out_ref[0, rows, pl.ds(h * gw + g * HEAD, HEAD)] = piece
            return carry

        pieces = 2 if h == 0 else 1
        for part in range(pieces):
            lax.fori_loop(
                part * blk_dev // pieces, (part + 1) * blk_dev // pieces, block_step, 0
            )
            if h < moved:
                hand_over(h, part, pieces).start()

        for i in range(2):
            for c in others:
                peer_copy(h, c, i).wait_send()
        forward(h, core).wait_send()
        if h + slots < moved:
            for c in others:
                pl.semaphore_signal(
                    free_c.at[s], inc=1, device_id={"seq": c * 2 + core}, device_id_type=MESH
                )
            pl.semaphore_signal(
                free_p.at[s], inc=1, device_id={"seq": partner}, device_id_type=MESH
            )
            start_gather(h + slots)

    for copy in shipped:
        copy.wait_send()
    for h in range(moved):
        hand_over(h, 0, 1).wait()


def write_out(x_ref, out_ref, sems):
    rows = out_ref.shape[1] // PIECES
    copies = [
        pltpu.make_async_copy(
            x_ref.at[:, pl.ds(i * rows, rows), :], out_ref.at[:, pl.ds(i * rows, rows), :], sems.at[i]
        )
        for i in range(PIECES)
    ]
    for copy in copies:
        copy.start()
    for copy in copies:
        copy.wait()


def per_device(queries, keys_in, values_in, random_blocks, global_blocks):
    n, segs = lax.axis_size("seq"), lax.axis_size("segment")
    tok, width = queries.shape[1:]
    kvh = keys_in.shape[2] // HEAD
    gw = width // kvh
    chips = n // 2
    blk_dev = tok // BLOCK
    slots = min(kvh - 1, max(2, SLOT_BYTES // (4 * n * tok * HEAD)))
    anywhere = pl.BlockSpec(memory_space=pl.ANY)
    scalars = pl.BlockSpec(memory_space=pltpu.SMEM)
    keys = (3 + GLOB + RAND) * BLOCK
    keys_in, values_in = (x.reshape(blk_dev, BLOCK, kvh * HEAD) for x in (keys_in, values_in))
    random_blocks = jnp.transpose(random_blocks, (2, 0, 1))
    landed = pl.pallas_call(
        functools.partial(kernel, n, segs, kvh, slots, min(2, slots)),
        out_shape=pltpu.VMEM(queries.shape, jnp.bfloat16),
        in_specs=[scalars] * 2 + [anywhere] * 5,
        out_specs=pl.BlockSpec(memory_space=pltpu.VMEM),
        scratch_shapes=[
            pltpu.VMEM((kvh, tok, gw), jnp.bfloat16),
            pltpu.VMEM((kvh - 1, tok, gw), jnp.bfloat16),
            pltpu.VMEM(random_blocks.shape, jnp.int32),
            pltpu.VMEM(global_blocks.shape, jnp.int32),
            pltpu.SMEM(random_blocks.shape, jnp.int32),
            pltpu.SMEM(global_blocks.shape, jnp.int32),
            *[
                pltpu.VMEM((4 * chips * blk_dev, BLOCK, HEAD), jnp.bfloat16)
                for _ in range(slots + 1)
            ],
            pltpu.SemaphoreType.DMA((kvh,)),
            pltpu.SemaphoreType.DMA((slots + 1, 2)),
            pltpu.SemaphoreType.DMA((slots + 1, chips, 2)),
            pltpu.SemaphoreType.DMA((slots + 1, chips, 2)),
            pltpu.SemaphoreType.DMA((slots + 1,)),
            pltpu.SemaphoreType.DMA((slots + 1,)),
            pltpu.SemaphoreType.DMA((kvh,)),
            pltpu.SemaphoreType.DMA((kvh,)),
            pltpu.SemaphoreType.DMA((5,)),
            pltpu.SemaphoreType.DMA((5,)),
            pltpu.SemaphoreType.DMA((2,)),
            pltpu.SemaphoreType.REGULAR((slots,)),
            pltpu.SemaphoreType.REGULAR((slots,)),
        ],
        compiler_params=pltpu.CompilerParams(
            collective_id=0, has_side_effects=True, vmem_limit_bytes=46 * 1024 * 1024
        ),
        cost_estimate=pl.CostEstimate(
            flops=4 * tok * width * keys,
            bytes_accessed=4 * tok * width,
            transcendentals=tok * width // HEAD * keys,
        ),
    )(random_blocks, global_blocks, random_blocks, global_blocks, queries, keys_in, values_in)
    return pl.pallas_call(
        write_out,
        out_shape=pltpu.HBM(queries.shape, jnp.bfloat16),
        in_specs=[pl.BlockSpec(memory_space=pltpu.VMEM)],
        out_specs=pl.BlockSpec(memory_space=pltpu.HBM),
        scratch_shapes=[pltpu.SemaphoreType.DMA((PIECES,))],
        compiler_params=pltpu.CompilerParams(vmem_limit_bytes=16 * 1024 * 1024),
        cost_estimate=pl.CostEstimate(
            flops=0, bytes_accessed=2 * tok * width, transcendentals=0
        ),
    )(pltpu.with_memory_space_constraint(landed, pltpu.VMEM))


def solution(mesh):
    in_specs = (
        P("segment", "seq", None),
        P("segment", "seq", None),
        P("segment", "seq", None),
        P("segment", "seq", None),
        P("segment", None),
    )
    out_specs = P("segment", "seq", None)
    return jax.shard_map(
        per_device, mesh=mesh, in_specs=in_specs, out_specs=out_specs, check_vma=False
    )
```
